256 devices in a mesh: queue: 64 (over z, y, core), head: 4 (over x).
Axes of the slice: x: 4, y: 4, z: 8, core: 2. Of those that a mesh axis runs over, the one named last changes fastest.
Arguments:
- latents: bfloat16 [12288, 1536], P('queue', 'head'), may hold values from -6 to 6
- fresh_frame: bfloat16 [384, 1536], P(None, 'head'), may hold values from -6 to 6
- noise_level: int32 [32], replicated, may hold values from 0 to 127, as said below
- offset: int32 [1], replicated, may hold values from 0 to 131071
- mod_table: float32 [128, 3, 1536], replicated, may hold values from -4 to 4
- w_qkv: bfloat16 [1536, 3, 1536], P(None, None, 'head'), may hold values from -1 to 1
- w_out: bfloat16 [1536, 1536], P('head'), may hold values from -0.15625 to 0.15625
- q_gain: float32 [1536], P('head'), may hold values from 1 to 3
- k_gain: float32 [1536], P('head'), may hold values from 1 to 3
Outputs:
- advanced: bfloat16 [12288, 1536], P('queue', 'head')
The draws below stay inside these ranges and needn't reach their ends.
Inputs may be any that keep to these rules, and one draw needn't show every extreme that they name: `noise_level`: entry p lies in p * 4 to (p + 1) * 4 - 1.
All inputs are finite; a program needn't handle non-finite values.
Results may differ from the reference program's by a relative error of at most 0.011.
Values may be sent and summed in bfloat16 or wider, within the bound.
No kernel may reach another device: no remote copies, remote signals or barrier semaphores. Data moves between devices by JAX's collectives and lax.ppermute only.
A program may use at most 128 MiB of HBM per device.

```python
import math
import jax
import jax.numpy as jnp
from jax import lax

D = 1536
HEADS = 12
DH = 128
TOK_DEV = 192
NOISE_STEP = 4
FRAMES = 32
FRAME_TOK = 384
TOKENS = 12288
LEVELS = 128


def draw_noise_level(key, part):
    key = jax.random.fold_in(key, 7)
    extra = jax.random.randint(key, (FRAMES,), 0, NOISE_STEP)
    index = jnp.arange(FRAMES, dtype=jnp.int32)
    extra = jnp.where(index == 0, 0, extra)
    extra = jnp.where(index == FRAMES - 1, NOISE_STEP - 1, extra)
    return (index * NOISE_STEP + extra).astype(jnp.int32)


def draw_w_qkv(key, part):
    key = jax.random.fold_in(key, 11)
    base_key = jax.random.fold_in(key, 0)
    weights = jnp.clip(jax.random.normal(base_key, (D, 3, D), jnp.float32), -4.0, 4.0) * D ** (-0.5)
    return jnp.clip(weights, -1.0, 1.0).astype(jnp.bfloat16)


def level_of(rng, shape, cuts, least, top_value):
    def one(dim, shards_of):
        steps = jax.random.uniform(jax.random.fold_in(jax.random.fold_in(rng, 6), dim), (shards_of,), jnp.float32, least / len(cuts), top_value / len(cuts))
        return jnp.repeat(jnp.exp(steps), shape[dim] // shards_of).reshape((-1,) + (1,) * (len(shape) - dim - 1))

    factor_of = one(*cuts[0])
    for cut in cuts[1:]:
        factor_of = factor_of * one(*cut)
    return factor_of


def scatter_about(own_key, shape, width, bound, cuts=(), kind=jnp.bfloat16):
    factor_of = level_of(own_key, shape, cuts, -0.22, 0.18) if cuts else 1.0
    entries = jax.random.normal(own_key, shape, jnp.float32) * width * factor_of
    return jnp.minimum(jnp.maximum(entries, -bound), bound).astype(kind)


def setup_inputs(seed: int = 0) -> dict:
    streams_of = jax.random.split(jax.random.key(seed), 10)
    latents = scatter_about(streams_of[0], (TOKENS, D), 1.0, 6.0, ((0, 64), (1, 4)))
    fresh_frame = scatter_about(streams_of[1], (FRAME_TOK, D), 1.0, 6.0, ((1, 4),))
    noise_level = draw_noise_level(jax.random.fold_in(streams_of[9], 71), 0)
    offset = jax.random.randint(streams_of[3], (1,), 0, FRAMES * 4096).astype(jnp.int32)
    mod_table = scatter_about(streams_of[4], (LEVELS, 3, D), 0.6, 4.0, (), jnp.float32)
    w_qkv = draw_w_qkv(jax.random.fold_in(streams_of[9], 71), 0)
    w_out = scatter_about(streams_of[6], (D, D), D ** -0.5, 0.15625, ((0, 4),))
    q_gain = jnp.clip(jnp.exp(math.log(3.0) - 1.0986123 * jax.random.uniform(streams_of[7], (D,), jnp.float32) ** level_of(streams_of[7], (D,), ((0, 4),), -0.2, 0.2)), 1.0, 3.0)
    k_gain = jnp.clip(jnp.exp(math.log(3.0) - 1.0986123 * jax.random.uniform(streams_of[8], (D,), jnp.float32) ** level_of(streams_of[8], (D,), ((0, 4),), -0.2, 0.2)), 1.0, 3.0)
    return {"latents": latents, "fresh_frame": fresh_frame, "noise_level": noise_level, "offset": offset, "mod_table": mod_table, "w_qkv": w_qkv, "w_out": w_out, "q_gain": q_gain, "k_gain": k_gain}


def reference(latents, fresh_frame, noise_level, offset, mod_table, w_qkv, w_out, q_gain, k_gain):
    slots = jnp.arange(FRAMES, dtype=jnp.int32)
    position = jnp.mod(slots - offset[0], FRAMES).astype(jnp.int32)
    levels = noise_level[position]
    modulation = mod_table[levels]
    whole = latents.astype(jnp.float32).reshape(FRAMES, FRAME_TOK, D)
    centered = whole - lax.optimization_barrier(jnp.mean(whole, axis=2, keepdims=True))
    variance = lax.optimization_barrier(jnp.mean(centered * centered, axis=2, keepdims=True))
    normed = centered * lax.rsqrt(variance + 1e-06)
    modded = (normed * (1.0 + modulation[:, 1][:, None, :]) + modulation[:, 0][:, None, :]).astype(jnp.bfloat16)
    modded = modded.reshape(TOKENS, D)
    projected = jnp.dot(modded, w_qkv.reshape(D, 3 * D), preferred_element_type=jnp.float32).reshape(TOKENS, 3, D)
    query_raw = projected[:, 0]
    key_raw = projected[:, 1]
    values = projected[:, 2].astype(jnp.bfloat16)
    queries = (query_raw * lax.rsqrt(lax.optimization_barrier(jnp.mean(query_raw * query_raw, axis=1, keepdims=True)) + 1e-06) * q_gain).astype(jnp.bfloat16)
    key_normed = (key_raw * lax.rsqrt(lax.optimization_barrier(jnp.mean(key_raw * key_raw, axis=1, keepdims=True)) + 1e-06) * k_gain).astype(jnp.bfloat16)
    query_blocks = queries.reshape(2 * FRAMES, TOK_DEV, HEADS, DH)
    block_position = jnp.repeat(position, 2)
    key_heads = key_normed.astype(jnp.float32).reshape(TOKENS, HEADS, DH)
    value_heads = values.astype(jnp.float32).reshape(TOKENS, HEADS, DH)
    key_position = jnp.repeat(position, FRAME_TOK)

    def one_block(operands):
        query_block, query_pos = operands
        scores = jnp.einsum('qhd,khd->hqk', query_block.astype(jnp.float32), key_heads) * DH ** (-0.5)
        allowed = key_position <= query_pos
        scores = jnp.where(allowed[None, None, :], scores, -jnp.inf)
        top_score = lax.optimization_barrier(jnp.max(scores, axis=2, keepdims=True))
        exp_scores = jnp.exp(scores - top_score)
        total = lax.optimization_barrier(jnp.sum(exp_scores, axis=2))
        rounded = lax.optimization_barrier(exp_scores.astype(jnp.bfloat16)).astype(jnp.float32)
        numer = jnp.einsum('hqk,khd->hqd', rounded, value_heads)
        result = numer / total[:, :, None]
        return jnp.transpose(result, (1, 0, 2)).reshape(TOK_DEV, D).astype(jnp.bfloat16)
    attn = lax.map(one_block, (query_blocks, block_position)).reshape(TOKENS, D)
    proj = jnp.dot(attn, w_out, preferred_element_type=jnp.float32).reshape(FRAMES, FRAME_TOK, D)
    updated = (whole + modulation[:, 2][:, None, :] * proj).astype(jnp.bfloat16)
    moved = jnp.roll(updated, -1, axis=0)
    fresh_slot = jnp.mod(offset[0] - 1, FRAMES)
    advanced = jnp.where((slots == fresh_slot)[:, None, None], fresh_frame[None, :, :], moved)
    return advanced.reshape(TOKENS, D)
```

```python
import functools

import jax
import jax.numpy as jnp
from jax import lax
from jax.experimental import pallas as pl
from jax.experimental.pallas import tpu as pltpu
from jax.sharding import PartitionSpec as P

D = 1536
DH = 128
LOG2E = 1.4426950408889634
LOW = -1e30
NY = 4
NZ = 8
TAIL = 16

VMEM = pl.BlockSpec(memory_space=pltpu.VMEM)
SMEM = pl.BlockSpec(memory_space=pltpu.SMEM)
PARAMS = pltpu.CompilerParams(vmem_limit_bytes=40 * 1024 * 1024)


def shift(block, axis, distance):
    n = lax.axis_size(axis)
    return lax.ppermute(block, axis, [((i - distance) % n, i) for i in range(n)])


def to_column(row, rows):
    pad = jnp.zeros((128 - row.shape[0], rows), row.dtype)
    return jnp.concatenate([row, pad], axis=0).T


def to_row(column):
    return column.T[0:8]


def lanes_of(columns, rows):
    lane = lax.broadcasted_iota(jnp.int32, (rows, 128), 1)
    out = jnp.zeros((rows, 128), jnp.float32)
    for j, column in enumerate(columns):
        out = jnp.where(lane == j, column, out)
    return out


def project_kernel(x_ref, own, one, two, three, scale_ref, shift_ref, w_ref, q_ref, k_ref, v_ref, sums_ref):
    x = x_ref[0]
    n = 4
    order = [lax.rem(x - j + n, n) for j in range(n)]
    width = own.shape[1]
    rows = own.shape[0]
    chunks = [r[...].astype(jnp.float32) for r in (own, one, two, three)]
    total = sum(jnp.sum(c, axis=1, keepdims=True) for c in chunks)
    mean = total / D
    centered = [c - mean for c in chunks]
    variance = sum(jnp.sum(c * c, axis=1, keepdims=True) for c in centered) / D
    inv = lax.rsqrt(variance + 1e-06)
    modded = []
    for j in range(n):
        sc = scale_ref[order[j]]
        sh = shift_ref[order[j]]
        modded.append((centered[j] * inv * (1.0 + sc) + sh).astype(jnp.bfloat16))
    outs = []
    for part in range(3):
        acc = None
        for j in range(n):
            start = pl.multiple_of(order[j] * width, 128)
            d = jnp.dot(modded[j], w_ref[part, pl.ds(start, width), :], preferred_element_type=jnp.float32)
            acc = d if acc is None else acc + d
        outs.append(acc)
    q_ref[...] = outs[0]
    k_ref[...] = outs[1]
    v_ref[...] = outs[2].astype(jnp.bfloat16)
    sums = [jnp.sum(o * o, axis=1, keepdims=True) for o in outs[:2]]
    sums_ref[...] = to_row(lanes_of(sums, rows))


def norm_kernel(q_ref, k_ref, v_ref, s0, s1, s2, s3, qg_ref, kg_ref, qn_ref, kv_ref):
    rows = q_ref.shape[0]
    total = s0[...] + s1[...] + s2[...] + s3[...]
    inv = to_column(lax.rsqrt(total / D + 1e-06), rows)
    qn_ref[...] = (q_ref[...] * inv[:, 0:1] * (qg_ref[...] * (LOG2E * DH ** (-0.5)))).astype(jnp.bfloat16)
    kv_ref[0] = (k_ref[...] * inv[:, 1:2] * kg_ref[...]).astype(jnp.bfloat16)
    kv_ref[1] = v_ref[...]


def attend_kernel(slabs, first, last, *refs):
    flags, qa, qb = refs[:3]
    at = 3
    keys, values = [], []
    for kind in slabs:
        if kind == 1:
            keys.append(refs[at].at[0])
            values.append(refs[at].at[1])
            at += 1
        else:
            keys.append(refs[at])
            values.append(refs[at + 1])
            at += 2
    if not first:
        acc_in, stat_in = refs[at], refs[at + 1]
        at += 2
    outs = refs[at:]
    rows = qa.shape[1]
    count = len(slabs)
    width = qa.shape[2]
    heads = width // DH
    col = lax.broadcasted_iota(jnp.int32, (1, rows * count), 1)
    ones = jnp.ones((rows * count, DH), jnp.bfloat16)

    def one_slab(q_ref, parity, k):
        bias = jnp.zeros((1, rows * count), jnp.float32)
        for j in range(count):
            inside = (col >= j * rows) & (col < (j + 1) * rows)
            bias = bias + jnp.where(inside, flags[k * count + j], 0.0)
        maxes, totals, accs = [], [], []
        stat = None if first else stat_in[parity * NY + k]
        for h in range(heads):
            lanes = slice(h * DH, (h + 1) * DH)
            q = q_ref[k, :, lanes]
            kk = jnp.concatenate([r[:, lanes] for r in keys], axis=0)
            vv = jnp.concatenate([r[:, lanes] for r in values], axis=0)
            s = lax.dot_general(q, kk, (((1,), (1,)), ((), ())), preferred_element_type=jnp.float32)
            s = s + bias
            top = jnp.max(s, axis=1, keepdims=True)
            if not first:
                old = stat[:, h : h + 1]
                top = jnp.maximum(top, old)
            e = jnp.exp2(s - top).astype(jnp.bfloat16)
            o = jnp.dot(e, jnp.concatenate([vv, ones], axis=1), preferred_element_type=jnp.float32)
            acc, tot = o[:, :DH], o[:, DH : DH + 1]
            if not first:
                fade = jnp.exp2(old - top)
                acc = acc + fade * acc_in[parity * NY + k, :, lanes]
                tot = tot + fade * stat[:, heads + h : heads + h + 1]
            maxes.append(top)
            totals.append(tot)
            accs.append(acc)
        if last:
            out = outs[parity]
            logs = []
            for h in range(heads):
                out[k, 0:rows, h * DH : (h + 1) * DH] = (accs[h] / totals[h]).astype(jnp.bfloat16)
                logs.append(maxes[h] + jnp.log2(totals[h]))
            out[k, rows : rows + TAIL, :] = pack_logs(to_row(lanes_of(logs, rows)), width)
        else:
            acc_out, stat_out = outs
            for h in range(heads):
                acc_out[parity * NY + k, :, h * DH : (h + 1) * DH] = accs[h]
            stat_out[parity * NY + k] = lanes_of(maxes + totals, rows)

    def step(k, carry):
        one_slab(qa, 0, k)
        one_slab(qb, 1, k)
        return carry

    lax.fori_loop(0, NY, step, 0)


def pack_logs(row, width):
    high = row.astype(jnp.bfloat16)
    low = (row - high.astype(jnp.float32)).astype(jnp.bfloat16)
    both = jnp.concatenate([high.astype(jnp.float32), low.astype(jnp.float32)], axis=0)
    pad = jnp.zeros((TAIL, width - row.shape[1]), jnp.float32)
    return jnp.concatenate([both, pad], axis=1).astype(jnp.bfloat16)


def merge(blocks, rows):
    logs = []
    for block in blocks:
        tail = block[rows : rows + TAIL, 0:rows].astype(jnp.float32)
        logs.append(tail[0:8] + tail[8:16])
    top = functools.reduce(jnp.maximum, logs)
    parts = [jnp.exp2(v - top) for v in logs]
    total = sum(parts)
    weights = [to_column(p / total, rows) for p in parts]
    heads = blocks[0].shape[1] // DH
    outs = []
    for h in range(heads):
        lanes = slice(h * DH, (h + 1) * DH)
        outs.append(
            sum(w[:, h : h + 1] * b[0:rows, lanes].astype(jnp.float32) for w, b in zip(weights, blocks, strict=True))
        )
    return outs, top + jnp.log2(total)


def pair_kernel(mine, other, out):
    rows = mine.shape[1] - TAIL
    for k in range(NY):
        outs, logs = merge([mine.at[k], other.at[k]], rows)
        for h, o in enumerate(outs):
            out[k, 0:rows, h * DH : (h + 1) * DH] = o.astype(jnp.bfloat16)
        out[k, rows : rows + TAIL, :] = pack_logs(logs, mine.shape[2])


def out_kernel(x_ref, a, b, c, d, w_ref, *outs):
    rows = a.shape[0] - TAIL
    width = a.shape[1]
    x = x_ref[0]
    parts, _ = merge([a, b, c, d], rows)
    attn = jnp.concatenate([p.astype(jnp.bfloat16) for p in parts], axis=1)
    n = len(outs)
    for j in range(n):
        start = pl.multiple_of(lax.rem(x + j, n) * width, 128)
        outs[j][...] = jnp.dot(attn, w_ref[:, pl.ds(start, width)], preferred_element_type=jnp.float32).astype(
            jnp.bfloat16
        )


def shape(dims, dtype):
    return jax.ShapeDtypeStruct(dims, dtype)


def call(kernel, ins, out_shape, flops, moved, exps=0):
    return pl.pallas_call(
        kernel,
        out_shape=out_shape,
        in_specs=ins,
        out_specs=jax.tree.map(lambda _: VMEM, out_shape),
        compiler_params=PARAMS,
        cost_estimate=pl.CostEstimate(flops=flops, bytes_accessed=moved, transcendentals=exps),
    )


def attend(flags, qa, qb, pieces, state, last):
    first = state is None
    slabs = tuple(1 if not isinstance(p, tuple) else 2 for p in pieces)
    flat = []
    for p in pieces:
        flat += list(p) if isinstance(p, tuple) else [p]
    slots, rows, width = qa.shape
    if last:
        out = [shape((slots, rows + TAIL, width), jnp.bfloat16)] * 2
    else:
        out = [shape((2 * slots, rows, width), jnp.float32), shape((2 * slots, rows, 128), jnp.float32)]
    scores = 2 * slots * rows * rows * len(slabs) * (width // DH)
    args = [flags, qa, qb, *flat] + ([] if first else list(state))
    return call(
        functools.partial(attend_kernel, slabs, first, last),
        [SMEM] + [VMEM] * (len(args) - 1),
        out,
        scores * DH * 4,
        4 << 20,
        scores,
    )(*args)


def local(latents, fresh_frame, noise_level, offset, mod_table, w_qkv, w_out, q_gain, k_gain):
    slabs = lax.axis_size("queue")
    frames = slabs // 2
    heads_ax = lax.axis_size("head")
    rows, width = latents.shape
    slab = lax.axis_index("queue")
    x = lax.axis_index("head")
    frame = slab // 2
    z, y = frame // NY, frame % NY
    x_arg = x.astype(jnp.int32).reshape(1)

    def place(f):
        return jnp.mod(f - offset[0], frames)

    chunks = [latents] + [shift(latents, "head", j) for j in range(1, heads_ax)]
    home_latents = shift(latents, "queue", -2)
    modulation = lax.dynamic_index_in_dim(mod_table, noise_level[place(frame)], 0, keepdims=False)
    home_level = noise_level[place(frame + 1)]
    gate = lax.dynamic_slice(mod_table, (home_level, 2, x * width), (1, 1, width)).reshape(1, width)
    modulation = modulation.reshape(3, heads_ax, 1, width)
    w3 = jnp.transpose(w_qkv, (1, 0, 2))
    q, k, v, sums = call(
        project_kernel,
        [SMEM] + [VMEM] * 7,
        [
            shape((rows, width), jnp.float32),
            shape((rows, width), jnp.float32),
            shape((rows, width), jnp.bfloat16),
            shape((8, rows), jnp.float32),
        ],
        2 * rows * D * 3 * width,
        6 << 20,
    )(x_arg, *chunks, modulation[1], modulation[0], w3)
    all_sums = [sums] + [shift(sums, "head", j) for j in range(1, heads_ax)]
    qn, kv = call(
        norm_kernel,
        [VMEM] * 9,
        [shape((rows, width), jnp.bfloat16), shape((2, rows, width), jnp.bfloat16)],
        rows * width * 8,
        2 << 20,
    )(q, k, v, *all_sums, q_gain.reshape(1, width), k_gain.reshape(1, width))

    def query_route(j):
        route = []
        for f in range(frames):
            fz, fy = f // NY, f % NY
            source = (fz * NY + (fy + j) % NY + 1) % frames
            route += [(2 * source + c, 2 * f + c) for c in range(2)]
        return route

    def key_route(distance):
        route = []
        for f in range(frames):
            fz, fy = f // NY, f % NY
            source = ((fz - distance) % NZ) * NY + fy
            route += [(2 * source + c, 2 * f + c) for c in range(2)]
        return route

    def y_route(distance):
        route = []
        for f in range(frames):
            fz, fy = f // NY, f % NY
            source = fz * NY + (fy - distance) % NY
            route += [(2 * source + c, 2 * f + c) for c in range(2)]
        return route

    swap = [(i, i ^ 1) for i in range(slabs)]

    def flags_of(distances):
        out = []
        for j in range(NY):
            q_place = place(z * NY + (y + j) % NY + 1)
            for d in distances:
                k_place = place(jnp.mod(z - d, NZ) * NY + y)
                out.append(jnp.where(k_place <= q_place, 0.0, LOW))
        return jnp.stack(out).astype(jnp.float32)

    up, down = kv, kv
    ups, downs = [kv], [kv]
    up = lax.ppermute(up, "queue", key_route(1))
    down = lax.ppermute(down, "queue", key_route(-1))
    qa = jnp.stack([lax.ppermute(qn, "queue", query_route(j)) for j in range(NY)])
    qb = lax.ppermute(qa, "queue", swap)
    ups.append(up)
    downs.append(down)
    for _ in range(2):
        ups.append(lax.ppermute(ups[-1], "queue", key_route(1)))
        downs.append(lax.ppermute(downs[-1], "queue", key_route(-1)))
    far_k = lax.ppermute(ups[3][0], "queue", key_route(1))
    far_v = lax.ppermute(downs[3][1], "queue", key_route(-1))

    state = attend(flags_of((0, 1, -1)), qa, qb, [kv, ups[1], downs[1]], None, False)
    state = attend(flags_of((2, -2)), qa, qb, [ups[2], downs[2]], state, False)
    state = attend(flags_of((3, -3)), qa, qb, [ups[3], downs[3]], state, False)
    mine, others = attend(flags_of((4,)), qa, qb, [(far_k, far_v)], state, True)

    received = lax.ppermute(others, "queue", swap)
    paired = call(
        pair_kernel, [VMEM] * 2, shape(mine.shape, jnp.bfloat16), mine.size * 4, mine.size * 6
    )(mine, received)
    parts = [paired[0]] + [lax.ppermute(paired[j], "queue", y_route(j)) for j in range(1, NY)]
    blocks = call(
        out_kernel,
        [SMEM] + [VMEM] * 5,
        [shape((rows, width), jnp.bfloat16)] * heads_ax,
        2 * rows * width * D,
        3 << 20,
    )(x_arg, *parts, w_out)
    proj = blocks[0].astype(jnp.float32)
    for j in range(1, heads_ax):
        proj = proj + shift(blocks[j], "head", j).astype(jnp.float32)
    updated = (home_latents.astype(jnp.float32) + gate * proj).astype(jnp.bfloat16)
    entry_slot = jnp.mod(offset[0] - 1, frames)
    fresh_half = lax.dynamic_slice_in_dim(fresh_frame, slab % 2 * rows, rows, 0)
    return jnp.where(frame == entry_slot, fresh_half, updated)


def solution(mesh):
    return jax.shard_map(
        local,
        mesh=mesh,
        in_specs=(
            P("queue", "head"),
            P(None, "head"),
            P(),
            P(),
            P(),
            P(None, None, "head"),
            P("head", None),
            P("head"),
            P("head"),
        ),
        out_specs=P("queue", "head"),
        check_vma=False,
    )
```

```python
import functools

import jax
import jax.numpy as jnp
from jax import lax
from jax.experimental import pallas as pl
from jax.experimental.pallas import tpu as pltpu
from jax.sharding import PartitionSpec as P

D = 1536
DH = 128
LOG2E = 1.4426950408889634
LOW = -1e30
NY = 4
NZ = 8
GROUPS = ((0, 1, -1, 2), (-2, 3, -3, 4))
TAIL = 16

VMEM = pl.BlockSpec(memory_space=pltpu.VMEM)
SMEM = pl.BlockSpec(memory_space=pltpu.SMEM)
MIB = 1024 * 1024


def shift(block, axis, distance):
    n = lax.axis_size(axis)
    return lax.ppermute(block, axis, [((i - distance) % n, i) for i in range(n)])


def to_column(row, rows):
    pad = jnp.zeros((128 - row.shape[0], rows), row.dtype)
    return jnp.concatenate([row, pad], axis=0).T


def to_row(column):
    return column.T[0:8]


def lanes_of(columns, rows):
    lane = lax.broadcasted_iota(jnp.int32, (rows, 128), 1)
    out = jnp.zeros((rows, 128), jnp.float32)
    for j, column in enumerate(columns):
        out = jnp.where(lane == j, column, out)
    return out


def project_kernel(x_ref, own, one, two, three, scale_ref, shift_ref, w_ref, q_ref, k_ref, v_ref, sums_ref):
    x = x_ref[0]
    n = 4
    order = [lax.rem(x - j + n, n) for j in range(n)]
    width = own.shape[1]
    rows = own.shape[0]
    chunks = [r[...].astype(jnp.float32) for r in (own, one, two, three)]
    total = sum(jnp.sum(c, axis=1, keepdims=True) for c in chunks)
    mean = total / D
    centered = [c - mean for c in chunks]
    variance = sum(jnp.sum(c * c, axis=1, keepdims=True) for c in centered) / D
    inv = lax.rsqrt(variance + 1e-06)
    modded = []
    for j in range(n):
        sc = scale_ref[order[j]]
        sh = shift_ref[order[j]]
        modded.append((centered[j] * inv * (1.0 + sc) + sh).astype(jnp.bfloat16))
    outs = []
    for part in range(3):
        acc = None
        for j in range(n):
            start = pl.multiple_of(order[j] * width, 128)
            d = jnp.dot(modded[j], w_ref[part, pl.ds(start, width), :], preferred_element_type=jnp.float32)
            acc = d if acc is None else acc + d
        outs.append(acc)
    q_ref[...] = outs[0]
    k_ref[...] = outs[1]
    v_ref[...] = outs[2].astype(jnp.bfloat16)
    sums = [jnp.sum(o * o, axis=1, keepdims=True) for o in outs[:2]]
    sums_ref[...] = to_row(lanes_of(sums, rows))


def norm_kernel(q_ref, k_ref, s0, s1, s2, s3, qg_ref, kg_ref, qn_ref, kn_ref):
    rows = q_ref.shape[0]
    total = s0[...] + s1[...] + s2[...] + s3[...]
    inv = to_column(lax.rsqrt(total / D + 1e-06), rows)
    qn_ref[...] = (q_ref[...] * inv[:, 0:1] * (qg_ref[...] * (LOG2E * DH ** (-0.5)))).astype(jnp.bfloat16)
    kn_ref[...] = (k_ref[...] * inv[:, 1:2] * kg_ref[...]).astype(jnp.bfloat16)


def attend_kernel(slabs, flags, *refs):
    queries, refs = refs[:NY], refs[NY:]
    keys, values, outs = refs[:slabs], refs[slabs : 2 * slabs], refs[2 * slabs :]
    rows, width = queries[0].shape[1:]
    heads = width // DH
    col = lax.broadcasted_iota(jnp.int32, (1, rows * slabs), 1)
    ones = jnp.ones((rows * slabs, DH), jnp.bfloat16)
    biases = []
    for k in range(NY):
        bias = jnp.full((1, rows * slabs), flags[k * slabs], jnp.float32)
        for j in range(1, slabs):
            bias = jnp.where(col >= j * rows, flags[k * slabs + j], bias)
        biases.append(bias)
    for parity, out in enumerate(outs):
        logs = [[] for _ in range(NY)]
        for h in range(heads):
            lanes = slice(h * DH, (h + 1) * DH)
            q = jnp.concatenate([r[parity, :, lanes] for r in queries], axis=0)
            kk = jnp.concatenate([r[:, lanes] for r in keys], axis=0)
            vv = jnp.concatenate([r[:, lanes] for r in values], axis=0)
            s = lax.dot_general(q, kk, (((1,), (1,)), ((), ())), preferred_element_type=jnp.float32)
            tops, es = [], []
            for k in range(NY):
                part = s[k * rows : (k + 1) * rows] + biases[k]
                top = jnp.max(part, axis=1, keepdims=True)
                es.append(jnp.exp2(part - top).astype(jnp.bfloat16))
                tops.append(top)
            e = jnp.concatenate(es, axis=0)
            o = jnp.dot(e, jnp.concatenate([vv, ones], axis=1), preferred_element_type=jnp.float32)
            for k in range(NY):
                here = slice(k * rows, (k + 1) * rows)
                total = o[here, DH:]
                out[k, 0:rows, lanes] = (o[here, :DH] / total).astype(jnp.bfloat16)
                logs[k].append(tops[k] + jnp.log2(total))
        for k in range(NY):
            out[k, rows : rows + TAIL, 0:rows] = log_rows(logs[k], rows)


def log_rows(columns, rows):
    lane = lax.broadcasted_iota(jnp.int32, (rows, 128), 1)
    tile = jnp.zeros((rows, 128), jnp.float32)
    for j, column in enumerate(columns):
        high = column.astype(jnp.bfloat16).astype(jnp.float32)
        tile = jnp.where(lane == j, high, jnp.where(lane == 8 + j, column - high, tile))
    pick = lax.broadcasted_iota(jnp.int32, (TAIL, 128), 0) == lax.broadcasted_iota(jnp.int32, (TAIL, 128), 1)
    out = lax.dot_general(
        pick.astype(jnp.bfloat16), tile.astype(jnp.bfloat16), (((1,), (1,)), ((), ())), preferred_element_type=jnp.float32
    )
    return out.astype(jnp.bfloat16)


def merge(blocks, rows):
    logs = []
    for block in blocks:
        tail = block[rows : rows + TAIL, 0:rows].astype(jnp.float32)
        logs.append(tail[0:8] + tail[8:16])
    width = blocks[0].shape[1]
    top = functools.reduce(jnp.maximum, logs)
    parts = [jnp.exp2(v - top) for v in logs]
    total = sum(parts)
    inv = 1.0 / total
    row = lax.broadcasted_iota(jnp.int32, (TAIL, width), 0) % 8
    spread = (row == lax.broadcasted_iota(jnp.int32, (TAIL, width), 1) // DH).astype(jnp.bfloat16)
    out = jnp.zeros((rows, width), jnp.float32)
    for part, block in zip(parts, blocks, strict=True):
        weight = part * inv
        high = weight.astype(jnp.bfloat16).astype(jnp.float32)
        both = jnp.concatenate([high, weight - high], axis=0).astype(jnp.bfloat16)
        column = lax.dot_general(both, spread, (((0,), (0,)), ((), ())), preferred_element_type=jnp.float32)
        out = out + column * block[0:rows, :].astype(jnp.float32)
    return out, top + jnp.log2(total)


def pair_kernel(*refs):
    blocks, out = refs[:-1], refs[-1]
    rows = out.shape[1] - TAIL
    for k in range(NY):
        merged, logs = merge([b.at[k] for b in blocks], rows)
        out[k, 0:rows, :] = merged.astype(jnp.bfloat16)
        high = logs.astype(jnp.bfloat16).astype(jnp.float32)
        both = jnp.concatenate([high, logs - high], axis=0)
        out[k, rows : rows + TAIL, 0:rows] = both.astype(jnp.bfloat16)


def out_kernel(x_ref, a, b, c, d, w_ref, *outs):
    rows = a.shape[0] - TAIL
    width = a.shape[1]
    x = x_ref[0]
    merged, _ = merge([a, b, c, d], rows)
    attn = merged.astype(jnp.bfloat16)
    n = len(outs)
    for j in range(n):
        start = pl.multiple_of(lax.rem(x + j, n) * width, 128)
        outs[j][...] = jnp.dot(attn, w_ref[:, pl.ds(start, width)], preferred_element_type=jnp.float32).astype(
            jnp.bfloat16
        )


def shape(dims, dtype):
    return jax.ShapeDtypeStruct(dims, dtype)


def call(kernel, ins, out_shape, flops, moved, exps=0):
    return pl.pallas_call(
        kernel,
        out_shape=out_shape,
        in_specs=ins,
        out_specs=jax.tree.map(lambda _: VMEM, out_shape),
        compiler_params=pltpu.CompilerParams(vmem_limit_bytes=40 * MIB),
        cost_estimate=pl.CostEstimate(flops=flops, bytes_accessed=moved, transcendentals=exps),
    )


def attend(flags, queries, keys, values):
    slots = len(queries)
    rows, width = queries[0].shape[1:]
    slabs = len(keys)
    scores = 2 * slots * rows * rows * slabs * (width // DH)
    return call(
        functools.partial(attend_kernel, slabs),
        [SMEM] + [VMEM] * (slots + 2 * slabs),
        [shape((slots, rows + TAIL, width), jnp.bfloat16)] * 2,
        scores * DH * 4,
        1 << 20,
        scores,
    )(flags, *queries, *keys, *values)


def combine(blocks):
    size = blocks[0].size
    return call(
        pair_kernel, [VMEM] * len(blocks), shape(blocks[0].shape, jnp.bfloat16), size * 2 * len(blocks), size * 2 * len(blocks)
    )(*blocks)


def local(latents, fresh_frame, noise_level, offset, mod_table, w_qkv, w_out, q_gain, k_gain):
    slabs = lax.axis_size("queue")
    frames = slabs // 2
    heads_ax = lax.axis_size("head")
    rows, width = latents.shape
    slab = lax.axis_index("queue")
    x = lax.axis_index("head")
    frame = slab // 2
    z, y = frame // NY, frame % NY
    x_arg = x.astype(jnp.int32).reshape(1)

    def place(f):
        return jnp.mod(f - offset[0], frames)

    chunks = [shift(latents, "head", j) for j in range(1, heads_ax)]
    home_latents = shift(latents, "queue", -2)
    modulation = lax.dynamic_index_in_dim(mod_table, noise_level[place(frame)], 0, keepdims=False)
    home_level = noise_level[place(frame + 1)]
    gate = lax.dynamic_slice(mod_table, (home_level, 2, x * width), (1, 1, width)).reshape(1, width)
    modulation = modulation.reshape(3, heads_ax, 1, width)
    w3 = jnp.transpose(w_qkv, (1, 0, 2))
    q, k, v, sums = call(
        project_kernel,
        [SMEM] + [VMEM] * 7,
        [
            shape((rows, width), jnp.float32),
            shape((rows, width), jnp.float32),
            shape((rows, width), jnp.bfloat16),
            shape((8, rows), jnp.float32),
        ],
        2 * rows * D * 3 * width,
        6 << 20,
    )(x_arg, latents, *chunks, modulation[1], modulation[0], w3)
    all_sums = [sums] + [shift(sums, "head", j) for j in range(1, heads_ax)]
    qn, kn = call(
        norm_kernel,
        [VMEM] * 8,
        [shape((rows, width), jnp.bfloat16)] * 2,
        rows * width * 8,
        2 << 20,
    )(q, k, *all_sums, q_gain.reshape(1, width), k_gain.reshape(1, width))

    def key_route(distance):
        route = []
        for f in range(frames):
            fz, fy = f // NY, f % NY
            source = ((fz - distance) % NZ) * NY + fy
            route += [(2 * source + c, 2 * f + c) for c in range(2)]
        return route

    def y_route(distance):
        route = []
        for f in range(frames):
            fz, fy = f // NY, f % NY
            source = fz * NY + (fy - distance) % NY
            route += [(2 * source + c, 2 * f + c) for c in range(2)]
        return route

    swap = [(i, i ^ 1) for i in range(slabs)]

    def flags_of(distances):
        out = []
        for j in range(NY):
            q_place = place(z * NY + (y + j) % NY + 1)
            for d in distances:
                k_place = place(jnp.mod(z - d, NZ) * NY + y)
                out.append(jnp.where(k_place <= q_place, 0.0, LOW))
        return jnp.stack(out).astype(jnp.float32)

    both = {0: jnp.stack([kn, v])}
    for way in (1, -1):
        both[way] = lax.ppermute(both[0], "queue", key_route(way))
    home_q = [shift(qn, "queue", -2), lax.ppermute(qn, "queue", [((i + 2) % slabs ^ 1, i) for i in range(slabs)])]
    both[1], both[-1], home_q = lax.optimization_barrier((both[1], both[-1], home_q))
    for way in (1, -1):
        both[way * 2] = lax.ppermute(both[way], "queue", key_route(way))
    home_q = jnp.stack(home_q)
    qs = [home_q] + [lax.ppermute(home_q, "queue", y_route(-j)) for j in range(1, NY)]
    for way in (1, -1):
        both[way * 3] = lax.ppermute(both[way * 2], "queue", key_route(way))
    ks = {d: b[0] for d, b in both.items()}
    vs = {d: b[1] for d, b in both.items()}

    def partial(distances):
        return attend(flags_of(distances), qs, [ks[d] for d in distances], [vs[d] for d in distances])

    ks[4] = lax.ppermute(ks[3], "queue", key_route(1))
    vs[4] = lax.ppermute(vs[-3], "queue", key_route(-1))
    ks[4], vs[4], home_latents = lax.optimization_barrier((ks[4], vs[4], home_latents))
    partials = [partial(distances) for distances in GROUPS]
    mine, other = [p[0] for p in partials], [p[1] for p in partials]
    received = lax.ppermute(combine(other), "queue", swap)
    paired = combine(mine + [received])
    parts = [paired[0]] + [lax.ppermute(paired[j], "queue", y_route(j)) for j in range(1, NY)]
    blocks = call(
        out_kernel,
        [SMEM] + [VMEM] * 5,
        [shape((rows, width), jnp.bfloat16)] * heads_ax,
        2 * rows * width * D,
        3 << 20,
    )(x_arg, *parts, w_out)
    proj = blocks[0].astype(jnp.float32)
    for j in range(1, heads_ax):
        proj = proj + shift(blocks[j], "head", j).astype(jnp.float32)
    updated = (home_latents.astype(jnp.float32) + gate * proj).astype(jnp.bfloat16)
    entry_slot = jnp.mod(offset[0] - 1, frames)
    fresh_half = lax.dynamic_slice_in_dim(fresh_frame, slab % 2 * rows, rows, 0)
    return jnp.where(frame == entry_slot, fresh_half, updated)


def solution(mesh):
    return jax.shard_map(
        local,
        mesh=mesh,
        in_specs=(
            P("queue", "head"),
            P(None, "head"),
            P(),
            P(),
            P(),
            P(None, None, "head"),
            P("head", None),
            P("head"),
            P("head"),
        ),
        out_specs=P("queue", "head"),
        check_vma=False,
    )
```

```python
import functools

import jax
import jax.numpy as jnp
from jax import lax
from jax.experimental import pallas as pl
from jax.experimental.pallas import tpu as pltpu
from jax.sharding import PartitionSpec as P

D = 1536
DH = 128
LOG2E = 1.4426950408889634
LOW = -1e30
NY = 4
NZ = 8
GROUPS = ((0, 1, -1, 2), (-2, 3, -3, 4))
TAIL = 16

VMEM = pl.BlockSpec(memory_space=pltpu.VMEM)
SMEM = pl.BlockSpec(memory_space=pltpu.SMEM)
MIB = 1024 * 1024


def shift(block, axis, distance):
    n = lax.axis_size(axis)
    return lax.ppermute(block, axis, [((i - distance) % n, i) for i in range(n)])


def to_column(row, rows):
    pad = jnp.zeros((128 - row.shape[0], rows), row.dtype)
    return jnp.concatenate([row, pad], axis=0).T


def to_row(column):
    return column.T[0:8]


def lanes_of(columns, rows):
    lane = lax.broadcasted_iota(jnp.int32, (rows, 128), 1)
    out = jnp.zeros((rows, 128), jnp.float32)
    for j, column in enumerate(columns):
        out = jnp.where(lane == j, column, out)
    return out


def early_kernel(w_in, w_out):
    w_out[...] = w_in[...]


def project_kernel(x_ref, own, one, two, three, scale_ref, shift_ref, w_ref, q_ref, k_ref, v_ref, sums_ref):
    x = x_ref[0]
    n = 4
    order = [lax.rem(x - j + n, n) for j in range(n)]
    width = own.shape[1]
    rows = own.shape[0]
    chunks = [r[...].astype(jnp.float32) for r in (own, one, two, three)]
    total = sum(jnp.sum(c, axis=1, keepdims=True) for c in chunks)
    mean = total / D
    centered = [c - mean for c in chunks]
    variance = sum(jnp.sum(c * c, axis=1, keepdims=True) for c in centered) / D
    inv = lax.rsqrt(variance + 1e-06)
    modded = []
    for j in range(n):
        sc = scale_ref[order[j]]
        sh = shift_ref[order[j]]
        modded.append((centered[j] * inv * (1.0 + sc) + sh).astype(jnp.bfloat16))
    outs = []
    for part in range(3):
        acc = None
        for j in range(n):
            start = pl.multiple_of(order[j] * width, 128)
            d = jnp.dot(modded[j], w_ref[part, pl.ds(start, width), :], preferred_element_type=jnp.float32)
            acc = d if acc is None else acc + d
        outs.append(acc)
    q_ref[...] = outs[0]
    k_ref[...] = outs[1]
    v_ref[...] = outs[2].astype(jnp.bfloat16)
    sums = [jnp.sum(o * o, axis=1, keepdims=True) for o in outs[:2]]
    sums_ref[...] = to_row(lanes_of(sums, rows))


def norm_kernel(q_ref, k_ref, s0, s1, s2, s3, qg_ref, kg_ref, qn_ref, kn_ref):
    rows = q_ref.shape[0]
    total = s0[...] + s1[...] + s2[...] + s3[...]
    inv = to_column(lax.rsqrt(total / D + 1e-06), rows)
    qn_ref[...] = (q_ref[...] * inv[:, 0:1] * (qg_ref[...] * (LOG2E * DH ** (-0.5)))).astype(jnp.bfloat16)
    kn_ref[...] = (k_ref[...] * inv[:, 1:2] * kg_ref[...]).astype(jnp.bfloat16)


def attend_kernel(slabs, flags, *refs):
    queries, refs = refs[:NY], refs[NY:]
    keys, values, outs = refs[:slabs], refs[slabs : 2 * slabs], refs[2 * slabs :]
    rows, width = queries[0].shape[1:]
    heads = width // DH
    col = lax.broadcasted_iota(jnp.int32, (1, rows * slabs), 1)
    ones = jnp.ones((rows * slabs, DH), jnp.bfloat16)
    biases = []
    for k in range(NY):
        bias = jnp.full((1, rows * slabs), flags[k * slabs], jnp.float32)
        for j in range(1, slabs):
            bias = jnp.where(col >= j * rows, flags[k * slabs + j], bias)
        biases.append(bias)
    for parity, out in enumerate(outs):
        logs = [[] for _ in range(NY)]
        for h in range(heads):
            lanes = slice(h * DH, (h + 1) * DH)
            q = jnp.concatenate([r[parity, :, lanes] for r in queries], axis=0)
            kk = jnp.concatenate([r[:, lanes] for r in keys], axis=0)
            vv = jnp.concatenate([r[:, lanes] for r in values], axis=0)
            s = lax.dot_general(q, kk, (((1,), (1,)), ((), ())), preferred_element_type=jnp.float32)
            tops, es = [], []
            for k in range(NY):
                part = s[k * rows : (k + 1) * rows] + biases[k]
                top = jnp.max(part, axis=1, keepdims=True)
                es.append(jnp.exp2(part - top).astype(jnp.bfloat16))
                tops.append(top)
            e = jnp.concatenate(es, axis=0)
            o = jnp.dot(e, jnp.concatenate([vv, ones], axis=1), preferred_element_type=jnp.float32)
            for k in range(NY):
                here = slice(k * rows, (k + 1) * rows)
                total = o[here, DH:]
                out[k, 0:rows, lanes] = (o[here, :DH] / total).astype(jnp.bfloat16)
                logs[k].append(tops[k] + jnp.log2(total))
        for k in range(NY):
            out[k, rows : rows + TAIL, 0:rows] = log_rows(logs[k], rows)


def log_rows(columns, rows):
    lane = lax.broadcasted_iota(jnp.int32, (rows, 128), 1)
    tile = jnp.zeros((rows, 128), jnp.float32)
    for j, column in enumerate(columns):
        high = column.astype(jnp.bfloat16).astype(jnp.float32)
        tile = jnp.where(lane == j, high, jnp.where(lane == 8 + j, column - high, tile))
    pick = lax.broadcasted_iota(jnp.int32, (TAIL, 128), 0) == lax.broadcasted_iota(jnp.int32, (TAIL, 128), 1)
    out = lax.dot_general(
        pick.astype(jnp.bfloat16), tile.astype(jnp.bfloat16), (((1,), (1,)), ((), ())), preferred_element_type=jnp.float32
    )
    return out.astype(jnp.bfloat16)


def merge(blocks, rows):
    logs = []
    for block in blocks:
        tail = block[rows : rows + TAIL, 0:rows].astype(jnp.float32)
        logs.append(tail[0:8] + tail[8:16])
    width = blocks[0].shape[1]
    top = functools.reduce(jnp.maximum, logs)
    parts = [jnp.exp2(v - top) for v in logs]
    total = sum(parts)
    inv = 1.0 / total
    row = lax.broadcasted_iota(jnp.int32, (TAIL, width), 0) % 8
    spread = (row == lax.broadcasted_iota(jnp.int32, (TAIL, width), 1) // DH).astype(jnp.bfloat16)
    out = jnp.zeros((rows, width), jnp.float32)
    for part, block in zip(parts, blocks, strict=True):
        weight = part * inv
        high = weight.astype(jnp.bfloat16).astype(jnp.float32)
        both = jnp.concatenate([high, weight - high], axis=0).astype(jnp.bfloat16)
        column = lax.dot_general(both, spread, (((0,), (0,)), ((), ())), preferred_element_type=jnp.float32)
        out = out + column * block[0:rows, :].astype(jnp.float32)
    return out, top + jnp.log2(total)


def pair_kernel(*refs):
    blocks, out = refs[:-1], refs[-1]
    rows = out.shape[1] - TAIL
    for k in range(NY):
        merged, logs = merge([b.at[k] for b in blocks], rows)
        out[k, 0:rows, :] = merged.astype(jnp.bfloat16)
        high = logs.astype(jnp.bfloat16).astype(jnp.float32)
        both = jnp.concatenate([high, logs - high], axis=0)
        out[k, rows : rows + TAIL, 0:rows] = both.astype(jnp.bfloat16)


def out_kernel(x_ref, a, b, c, d, w_ref, *outs):
    rows = a.shape[0] - TAIL
    width = a.shape[1]
    x = x_ref[0]
    merged, _ = merge([a, b, c, d], rows)
    attn = merged.astype(jnp.bfloat16)
    n = len(outs)
    for j in range(n):
        start = pl.multiple_of(lax.rem(x + j, n) * width, 128)
        outs[j][...] = jnp.dot(attn, w_ref[:, pl.ds(start, width)], preferred_element_type=jnp.float32).astype(
            jnp.bfloat16
        )


def shape(dims, dtype):
    return jax.ShapeDtypeStruct(dims, dtype)


def call(kernel, ins, out_shape, flops, moved, exps=0):
    return pl.pallas_call(
        kernel,
        out_shape=out_shape,
        in_specs=ins,
        out_specs=jax.tree.map(lambda _: VMEM, out_shape),
        compiler_params=pltpu.CompilerParams(vmem_limit_bytes=40 * MIB),
        cost_estimate=pl.CostEstimate(flops=flops, bytes_accessed=moved, transcendentals=exps),
    )


def attend(flags, queries, keys, values):
    slots = len(queries)
    rows, width = queries[0].shape[1:]
    slabs = len(keys)
    scores = 2 * slots * rows * rows * slabs * (width // DH)
    return call(
        functools.partial(attend_kernel, slabs),
        [SMEM] + [VMEM] * (slots + 2 * slabs),
        [shape((slots, rows + TAIL, width), jnp.bfloat16)] * 2,
        scores * DH * 14,
        1 << 20,
        scores,
    )(flags, *queries, *keys, *values)


def combine(blocks):
    size = blocks[0].size
    return call(
        pair_kernel, [VMEM] * len(blocks), shape(blocks[0].shape, jnp.bfloat16), size * 2 * len(blocks), size * 2 * len(blocks)
    )(*blocks)


def local(latents, fresh_frame, noise_level, offset, mod_table, w_qkv, w_out, q_gain, k_gain):
    slabs = lax.axis_size("queue")
    frames = slabs // 2
    heads_ax = lax.axis_size("head")
    rows, width = latents.shape
    slab = lax.axis_index("queue")
    x = lax.axis_index("head")
    frame = slab // 2
    z, y = frame // NY, frame % NY
    x_arg = x.astype(jnp.int32).reshape(1)

    def place(f):
        return jnp.mod(f - offset[0], frames)

    chunks = [shift(latents, "head", j) for j in range(1, heads_ax)]
    home_latents = shift(latents, "queue", -2)
    modulation = lax.dynamic_index_in_dim(mod_table, noise_level[place(frame)], 0, keepdims=False)
    home_level = noise_level[place(frame + 1)]
    gate = lax.dynamic_slice(mod_table, (home_level, 2, x * width), (1, 1, width)).reshape(1, width)
    modulation = modulation.reshape(3, heads_ax, 1, width)
    w3 = jnp.transpose(w_qkv, (1, 0, 2))
    w_near = call(early_kernel, [VMEM], shape(w3.shape, jnp.bfloat16), 0, 8 << 20)(w3)
    q, k, v, sums = call(
        project_kernel,
        [SMEM] + [VMEM] * 7,
        [
            shape((rows, width), jnp.float32),
            shape((rows, width), jnp.float32),
            shape((rows, width), jnp.bfloat16),
            shape((8, rows), jnp.float32),
        ],
        2 * rows * D * 3 * width,
        6 << 20,
    )(x_arg, latents, *chunks, modulation[1], modulation[0], w_near)
    all_sums = [sums] + [shift(sums, "head", j) for j in range(1, heads_ax)]
    qn, kn = call(
        norm_kernel,
        [VMEM] * 8,
        [shape((rows, width), jnp.bfloat16)] * 2,
        rows * width * 8,
        2 << 20,
    )(q, k, *all_sums, q_gain.reshape(1, width), k_gain.reshape(1, width))

    def key_route(distance):
        route = []
        for f in range(frames):
            fz, fy = f // NY, f % NY
            source = ((fz - distance) % NZ) * NY + fy
            route += [(2 * source + c, 2 * f + c) for c in range(2)]
        return route

    def y_route(distance):
        route = []
        for f in range(frames):
            fz, fy = f // NY, f % NY
            source = fz * NY + (fy - distance) % NY
            route += [(2 * source + c, 2 * f + c) for c in range(2)]
        return route

    swap = [(i, i ^ 1) for i in range(slabs)]

    def flags_of(distances):
        out = []
        for j in range(NY):
            q_place = place(z * NY + (y + j) % NY + 1)
            for d in distances:
                k_place = place(jnp.mod(z - d, NZ) * NY + y)
                out.append(jnp.where(k_place <= q_place, 0.0, LOW))
        return jnp.stack(out).astype(jnp.float32)

    both = {0: jnp.stack([kn, v])}
    for way in (1, -1):
        both[way] = lax.ppermute(both[0], "queue", key_route(way))
    home_q = [shift(qn, "queue", -2), lax.ppermute(qn, "queue", [((i + 2) % slabs ^ 1, i) for i in range(slabs)])]
    both[1], both[-1], home_q = lax.optimization_barrier((both[1], both[-1], home_q))
    for way in (1, -1):
        both[way * 2] = lax.ppermute(both[way], "queue", key_route(way))
    home_q = jnp.stack(home_q)
    qs = [home_q] + [lax.ppermute(home_q, "queue", y_route(-j)) for j in range(1, NY)]
    for way in (1, -1):
        both[way * 3] = lax.ppermute(both[way * 2], "queue", key_route(way))
    both[3], both[-3], qs = lax.optimization_barrier((both[3], both[-3], qs))
    ks = {d: b[0] for d, b in both.items()}
    vs = {d: b[1] for d, b in both.items()}

    def partial(distances):
        return attend(flags_of(distances), qs, [ks[d] for d in distances], [vs[d] for d in distances])

    ks[4] = lax.ppermute(ks[3], "queue", key_route(1))
    vs[4] = lax.ppermute(vs[-3], "queue", key_route(-1))
    ks[4], vs[4], home_latents = lax.optimization_barrier((ks[4], vs[4], home_latents))
    partials = [partial(distances) for distances in GROUPS]
    mine, other = [p[0] for p in partials], [p[1] for p in partials]
    received = lax.ppermute(combine(other), "queue", swap)
    paired = combine(mine + [received])
    parts = [paired[0]] + [lax.ppermute(paired[j], "queue", y_route(j)) for j in range(1, NY)]
    blocks = call(
        out_kernel,
        [SMEM] + [VMEM] * 5,
        [shape((rows, width), jnp.bfloat16)] * heads_ax,
        2 * rows * width * D,
        3 << 20,
    )(x_arg, *parts, w_out)
    proj = blocks[0].astype(jnp.float32)
    for j in range(1, heads_ax):
        proj = proj + shift(blocks[j], "head", j).astype(jnp.float32)
    updated = (home_latents.astype(jnp.float32) + gate * proj).astype(jnp.bfloat16)
    entry_slot = jnp.mod(offset[0] - 1, frames)
    fresh_half = lax.dynamic_slice_in_dim(fresh_frame, slab % 2 * rows, rows, 0)
    return jnp.where(frame == entry_slot, fresh_half, updated)


def solution(mesh):
    return jax.shard_map(
        local,
        mesh=mesh,
        in_specs=(
            P("queue", "head"),
            P(None, "head"),
            P(),
            P(),
            P(),
            P(None, None, "head"),
            P("head", None),
            P("head"),
            P("head"),
        ),
        out_specs=P("queue", "head"),
        check_vma=False,
    )
```

```python
import functools

import jax
import jax.numpy as jnp
from jax import lax
from jax.experimental import pallas as pl
from jax.experimental.pallas import tpu as pltpu
from jax.sharding import PartitionSpec as P

D = 1536
DH = 128
LOG2E = 1.4426950408889634
LOW = -1e30
NY = 4
NZ = 8
GROUPS = ((0, 1, -1, 2), (-2, 3, -3, 4))
TAIL = 16

VMEM = pl.BlockSpec(memory_space=pltpu.VMEM)
SMEM = pl.BlockSpec(memory_space=pltpu.SMEM)
MIB = 1024 * 1024


def shift(block, axis, distance):
    n = lax.axis_size(axis)
    return lax.ppermute(block, axis, [((i - distance) % n, i) for i in range(n)])


def to_column(row, rows):
    pad = jnp.zeros((128 - row.shape[0], rows), row.dtype)
    return jnp.concatenate([row, pad], axis=0).T


def to_row(column):
    return column.T[0:8]


def lanes_of(columns, rows):
    lane = lax.broadcasted_iota(jnp.int32, (rows, 128), 1)
    out = jnp.zeros((rows, 128), jnp.float32)
    for j, column in enumerate(columns):
        out = jnp.where(lane == j, column, out)
    return out


def early_kernel(w_in, w_out):
    w_out[...] = w_in[...]


def project_kernel(x_ref, own, one, two, three, scale_ref, shift_ref, w_ref, q_ref, k_ref, v_ref, sums_ref):
    x = x_ref[0]
    n = 4
    order = [lax.rem(x - j + n, n) for j in range(n)]
    width = own.shape[1]
    rows = own.shape[0]
    chunks = [r[...].astype(jnp.float32) for r in (own, one, two, three)]
    total = sum(jnp.sum(c, axis=1, keepdims=True) for c in chunks)
    mean = total / D
    centered = [c - mean for c in chunks]
    variance = sum(jnp.sum(c * c, axis=1, keepdims=True) for c in centered) / D
    inv = lax.rsqrt(variance + 1e-06)
    modded = []
    for j in range(n):
        sc = scale_ref[order[j]]
        sh = shift_ref[order[j]]
        modded.append((centered[j] * inv * (1.0 + sc) + sh).astype(jnp.bfloat16))
    outs = []
    for part in range(3):
        acc = None
        for j in range(n):
            start = pl.multiple_of(order[j] * width, 128)
            d = jnp.dot(modded[j], w_ref[part, pl.ds(start, width), :], preferred_element_type=jnp.float32)
            acc = d if acc is None else acc + d
        outs.append(acc)
    q_ref[...] = outs[0]
    k_ref[...] = outs[1]
    v_ref[...] = outs[2].astype(jnp.bfloat16)
    sums = [jnp.sum(o * o, axis=1, keepdims=True) for o in outs[:2]]
    sums_ref[...] = to_row(lanes_of(sums, rows))


def norm_kernel(q_ref, k_ref, s0, s1, s2, s3, qg_ref, kg_ref, qn_ref, kn_ref):
    rows = q_ref.shape[0]
    total = s0[...] + s1[...] + s2[...] + s3[...]
    inv = to_column(lax.rsqrt(total / D + 1e-06), rows)
    qn_ref[...] = (q_ref[...] * inv[:, 0:1] * (qg_ref[...] * (LOG2E * DH ** (-0.5)))).astype(jnp.bfloat16)
    kn_ref[...] = (k_ref[...] * inv[:, 1:2] * kg_ref[...]).astype(jnp.bfloat16)


def attend_kernel(slabs, flags, *refs):
    queries, refs = refs[:NY], refs[NY:]
    keys, values, outs = refs[:slabs], refs[slabs : 2 * slabs], refs[2 * slabs :]
    rows, width = queries[0].shape[1:]
    heads = width // DH
    col = lax.broadcasted_iota(jnp.int32, (1, rows * slabs), 1)
    ones = jnp.ones((rows * slabs, DH), jnp.bfloat16)
    biases = []
    for k in range(NY):
        bias = jnp.full((1, rows * slabs), flags[k * slabs], jnp.float32)
        for j in range(1, slabs):
            bias = jnp.where(col >= j * rows, flags[k * slabs + j], bias)
        biases.append(bias)
    for parity, out in enumerate(outs):
        logs = [[] for _ in range(NY)]
        for h in range(heads):
            lanes = slice(h * DH, (h + 1) * DH)
            q = jnp.concatenate([r[parity, :, lanes] for r in queries], axis=0)
            kk = jnp.concatenate([r[:, lanes] for r in keys], axis=0)
            vv = jnp.concatenate([r[:, lanes] for r in values], axis=0)
            s = lax.dot_general(q, kk, (((1,), (1,)), ((), ())), preferred_element_type=jnp.float32)
            tops, es = [], []
            for k in range(NY):
                part = s[k * rows : (k + 1) * rows] + biases[k]
                top = jnp.max(part, axis=1, keepdims=True)
                es.append(jnp.exp2(part - top).astype(jnp.bfloat16))
                tops.append(top)
            e = jnp.concatenate(es, axis=0)
            o = jnp.dot(e, jnp.concatenate([vv, ones], axis=1), preferred_element_type=jnp.float32)
            for k in range(NY):
                here = slice(k * rows, (k + 1) * rows)
                total = o[here, DH:]
                out[k, 0:rows, lanes] = (o[here, :DH] / total).astype(jnp.bfloat16)
                logs[k].append(tops[k] + jnp.log2(total))
        for k in range(NY):
            out[k, rows : rows + TAIL, 0:rows] = log_rows(logs[k], rows)


def log_rows(columns, rows):
    lane = lax.broadcasted_iota(jnp.int32, (rows, 128), 1)
    tile = jnp.zeros((rows, 128), jnp.float32)
    for j, column in enumerate(columns):
        high = column.astype(jnp.bfloat16).astype(jnp.float32)
        tile = jnp.where(lane == j, high, jnp.where(lane == 8 + j, column - high, tile))
    pick = lax.broadcasted_iota(jnp.int32, (TAIL, 128), 0) == lax.broadcasted_iota(jnp.int32, (TAIL, 128), 1)
    out = lax.dot_general(
        pick.astype(jnp.bfloat16), tile.astype(jnp.bfloat16), (((1,), (1,)), ((), ())), preferred_element_type=jnp.float32
    )
    return out.astype(jnp.bfloat16)


def merge(blocks, rows):
    logs = []
    for block in blocks:
        tail = block[rows : rows + TAIL, 0:rows].astype(jnp.float32)
        logs.append(tail[0:8] + tail[8:16])
    width = blocks[0].shape[1]
    top = functools.reduce(jnp.maximum, logs)
    parts = [jnp.exp2(v - top) for v in logs]
    total = sum(parts)
    inv = 1.0 / total
    row = lax.broadcasted_iota(jnp.int32, (TAIL, width), 0) % 8
    spread = (row == lax.broadcasted_iota(jnp.int32, (TAIL, width), 1) // DH).astype(jnp.bfloat16)
    out = jnp.zeros((rows, width), jnp.float32)
    for part, block in zip(parts, blocks, strict=True):
        weight = part * inv
        high = weight.astype(jnp.bfloat16).astype(jnp.float32)
        both = jnp.concatenate([high, weight - high], axis=0).astype(jnp.bfloat16)
        column = lax.dot_general(both, spread, (((0,), (0,)), ((), ())), preferred_element_type=jnp.float32)
        out = out + column * block[0:rows, :].astype(jnp.float32)
    return out, top + jnp.log2(total)


def pair_kernel(*refs):
    blocks, out = refs[:-1], refs[-1]
    rows = out.shape[1] - TAIL
    for k in range(NY):
        merged, logs = merge([b.at[k] for b in blocks], rows)
        out[k, 0:rows, :] = merged.astype(jnp.bfloat16)
        high = logs.astype(jnp.bfloat16).astype(jnp.float32)
        both = jnp.concatenate([high, logs - high], axis=0)
        out[k, rows : rows + TAIL, 0:rows] = both.astype(jnp.bfloat16)


def out_kernel(x_ref, a, b, c, d, w_ref, *outs):
    rows = a.shape[0] - TAIL
    width = a.shape[1]
    x = x_ref[0]
    merged, _ = merge([a, b, c, d], rows)
    attn = merged.astype(jnp.bfloat16)
    n = len(outs)
    for j in range(n):
        start = pl.multiple_of(lax.rem(x + j, n) * width, 128)
        outs[j][...] = jnp.dot(attn, w_ref[:, pl.ds(start, width)], preferred_element_type=jnp.float32).astype(
            jnp.bfloat16
        )


def shape(dims, dtype):
    return jax.ShapeDtypeStruct(dims, dtype)


def call(kernel, ins, out_shape, flops, moved, exps=0):
    return pl.pallas_call(
        kernel,
        out_shape=out_shape,
        in_specs=ins,
        out_specs=jax.tree.map(lambda _: VMEM, out_shape),
        compiler_params=pltpu.CompilerParams(vmem_limit_bytes=40 * MIB),
        cost_estimate=pl.CostEstimate(flops=flops, bytes_accessed=moved, transcendentals=exps),
    )


def attend(flags, queries, keys, values):
    slots = len(queries)
    rows, width = queries[0].shape[1:]
    slabs = len(keys)
    scores = 2 * slots * rows * rows * slabs * (width // DH)
    return call(
        functools.partial(attend_kernel, slabs),
        [SMEM] + [VMEM] * (slots + 2 * slabs),
        [shape((slots, rows + TAIL, width), jnp.bfloat16)] * 2,
        scores * DH * 14,
        1 << 20,
        scores,
    )(flags, *queries, *keys, *values)


def combine(blocks):
    size = blocks[0].size
    return call(
        pair_kernel, [VMEM] * len(blocks), shape(blocks[0].shape, jnp.bfloat16), size * 2 * len(blocks), size * 2 * len(blocks)
    )(*blocks)


def local(latents, fresh_frame, noise_level, offset, mod_table, w_qkv, w_out, q_gain, k_gain):
    slabs = lax.axis_size("queue")
    frames = slabs // 2
    heads_ax = lax.axis_size("head")
    rows, width = latents.shape
    slab = lax.axis_index("queue")
    x = lax.axis_index("head")
    frame = slab // 2
    z, y = frame // NY, frame % NY
    x_arg = x.astype(jnp.int32).reshape(1)

    def place(f):
        return jnp.mod(f - offset[0], frames)

    chunks = [shift(latents, "head", j) for j in range(1, heads_ax)]
    home_latents = shift(latents, "queue", -2)
    w3 = jnp.transpose(w_qkv, (1, 0, 2))
    w_near = call(early_kernel, [VMEM], shape(w3.shape, jnp.bfloat16), 0, 8 << 20)(w3)
    w_near, noise_level = lax.optimization_barrier((w_near, noise_level))
    modulation = lax.dynamic_index_in_dim(mod_table, noise_level[place(frame)], 0, keepdims=False)
    home_level = noise_level[place(frame + 1)]
    gate = lax.dynamic_slice(mod_table, (home_level, 2, x * width), (1, 1, width)).reshape(1, width)
    modulation = modulation.reshape(3, heads_ax, 1, width)
    q, k, v, sums = call(
        project_kernel,
        [SMEM] + [VMEM] * 7,
        [
            shape((rows, width), jnp.float32),
            shape((rows, width), jnp.float32),
            shape((rows, width), jnp.bfloat16),
            shape((8, rows), jnp.float32),
        ],
        2 * rows * D * 3 * width,
        6 << 20,
    )(x_arg, latents, *chunks, modulation[1], modulation[0], w_near)
    all_sums = [sums] + [shift(sums, "head", j) for j in range(1, heads_ax)]
    all_sums, home_latents = lax.optimization_barrier((all_sums, home_latents))
    qn, kn = call(
        norm_kernel,
        [VMEM] * 8,
        [shape((rows, width), jnp.bfloat16)] * 2,
        rows * width * 8,
        2 << 20,
    )(q, k, *all_sums, q_gain.reshape(1, width), k_gain.reshape(1, width))

    def key_route(distance):
        route = []
        for f in range(frames):
            fz, fy = f // NY, f % NY
            source = ((fz - distance) % NZ) * NY + fy
            route += [(2 * source + c, 2 * f + c) for c in range(2)]
        return route

    def y_route(distance):
        route = []
        for f in range(frames):
            fz, fy = f // NY, f % NY
            source = fz * NY + (fy - distance) % NY
            route += [(2 * source + c, 2 * f + c) for c in range(2)]
        return route

    swap = [(i, i ^ 1) for i in range(slabs)]

    def flags_of(distances):
        out = []
        for j in range(NY):
            q_place = place(z * NY + (y + j) % NY + 1)
            for d in distances:
                k_place = place(jnp.mod(z - d, NZ) * NY + y)
                out.append(jnp.where(k_place <= q_place, 0.0, LOW))
        return jnp.stack(out).astype(jnp.float32)

    both = {0: jnp.stack([kn, v])}
    for way in (1, -1):
        both[way] = lax.ppermute(both[0], "queue", key_route(way))
    home_q = [shift(qn, "queue", -2), lax.ppermute(qn, "queue", [((i + 2) % slabs ^ 1, i) for i in range(slabs)])]
    both[1], both[-1], home_q = lax.optimization_barrier((both[1], both[-1], home_q))
    for way in (1, -1):
        both[way * 2] = lax.ppermute(both[way], "queue", key_route(way))
    home_q = jnp.stack(home_q)
    qs = [home_q] + [lax.ppermute(home_q, "queue", y_route(-j)) for j in range(1, NY)]
    for way in (1, -1):
        both[way * 3] = lax.ppermute(both[way * 2], "queue", key_route(way))
    both[3], both[-3], qs = lax.optimization_barrier((both[3], both[-3], qs))
    ks = {d: b[0] for d, b in both.items()}
    vs = {d: b[1] for d, b in both.items()}

    def partial(distances):
        return attend(flags_of(distances), qs, [ks[d] for d in distances], [vs[d] for d in distances])

    ks[4] = lax.ppermute(ks[3], "queue", key_route(1))
    vs[4] = lax.ppermute(vs[-3], "queue", key_route(-1))
    partials = [partial(distances) for distances in GROUPS]
    mine, other = [p[0] for p in partials], [p[1] for p in partials]
    received = lax.ppermute(combine(other), "queue", swap)
    paired = combine(mine + [received])
    parts = [paired[0]] + [lax.ppermute(paired[j], "queue", y_route(j)) for j in range(1, NY)]
    blocks = call(
        out_kernel,
        [SMEM] + [VMEM] * 5,
        [shape((rows, width), jnp.bfloat16)] * heads_ax,
        2 * rows * width * D,
        3 << 20,
    )(x_arg, *parts, w_out)
    proj = blocks[0].astype(jnp.float32)
    for j in range(1, heads_ax):
        proj = proj + shift(blocks[j], "head", j).astype(jnp.float32)
    updated = (home_latents.astype(jnp.float32) + gate * proj).astype(jnp.bfloat16)
    entry_slot = jnp.mod(offset[0] - 1, frames)
    fresh_half = lax.dynamic_slice_in_dim(fresh_frame, slab % 2 * rows, rows, 0)
    return jnp.where(frame == entry_slot, fresh_half, updated)


def solution(mesh):
    return jax.shard_map(
        local,
        mesh=mesh,
        in_specs=(
            P("queue", "head"),
            P(None, "head"),
            P(),
            P(),
            P(),
            P(None, None, "head"),
            P("head", None),
            P("head"),
            P("head"),
        ),
        out_specs=P("queue", "head"),
        check_vma=False,
    )
```

```python
import functools

import jax
import jax.numpy as jnp
from jax import lax
from jax.experimental import pallas as pl
from jax.experimental.pallas import tpu as pltpu
from jax.sharding import PartitionSpec as P

D = 1536
DH = 128
LOG2E = 1.4426950408889634
LOW = -1e30
NY = 4
NZ = 8
GROUPS = ((0, 1, -1, 2), (-2, 3, -3, 4))
TAIL = 16

VMEM = pl.BlockSpec(memory_space=pltpu.VMEM)
SMEM = pl.BlockSpec(memory_space=pltpu.SMEM)
MIB = 1024 * 1024


def shift(block, axis, distance):
    n = lax.axis_size(axis)
    return lax.ppermute(block, axis, [((i - distance) % n, i) for i in range(n)])


def to_column(row, rows):
    pad = jnp.zeros((128 - row.shape[0], rows), row.dtype)
    return jnp.concatenate([row, pad], axis=0).T


def to_row(column):
    return column.T[0:8]


def lanes_of(columns, rows):
    lane = lax.broadcasted_iota(jnp.int32, (rows, 128), 1)
    out = jnp.zeros((rows, 128), jnp.float32)
    for j, column in enumerate(columns):
        out = jnp.where(lane == j, column, out)
    return out


def early_kernel(w_in, w_out):
    w_out[...] = w_in[...]


def project_kernel(x_ref, own, one, two, three, scale_ref, shift_ref, w_ref, q_ref, k_ref, v_ref, sums_ref):
    x = x_ref[0]
    n = 4
    order = [lax.rem(x - j + n, n) for j in range(n)]
    width = own.shape[1]
    rows = own.shape[0]
    chunks = [r[...].astype(jnp.float32) for r in (own, one, two, three)]
    total = sum(jnp.sum(c, axis=1, keepdims=True) for c in chunks)
    mean = total / D
    centered = [c - mean for c in chunks]
    variance = sum(jnp.sum(c * c, axis=1, keepdims=True) for c in centered) / D
    inv = lax.rsqrt(variance + 1e-06)
    modded = []
    for j in range(n):
        sc = scale_ref[order[j]]
        sh = shift_ref[order[j]]
        modded.append((centered[j] * inv * (1.0 + sc) + sh).astype(jnp.bfloat16))
    outs = []
    for part in range(3):
        acc = None
        for j in range(n):
            start = pl.multiple_of(order[j] * width, 128)
            d = jnp.dot(modded[j], w_ref[part, pl.ds(start, width), :], preferred_element_type=jnp.float32)
            acc = d if acc is None else acc + d
        outs.append(acc)
    q_ref[...] = outs[0]
    k_ref[...] = outs[1]
    v_ref[...] = outs[2].astype(jnp.bfloat16)
    sums = [jnp.sum(o * o, axis=1, keepdims=True) for o in outs[:2]]
    sums_ref[...] = to_row(lanes_of(sums, rows))


def norm_kernel(q_ref, k_ref, s0, s1, s2, s3, qg_ref, kg_ref, qn_ref, kn_ref):
    rows = q_ref.shape[0]
    total = s0[...] + s1[...] + s2[...] + s3[...]
    inv = to_column(lax.rsqrt(total / D + 1e-06), rows)
    qn_ref[...] = (q_ref[...] * inv[:, 0:1] * (qg_ref[...] * (LOG2E * DH ** (-0.5)))).astype(jnp.bfloat16)
    kn_ref[...] = (k_ref[...] * inv[:, 1:2] * kg_ref[...]).astype(jnp.bfloat16)


def attend_kernel(slabs, flags, *refs):
    queries, refs = refs[:NY], refs[NY:]
    keys, values, outs = refs[:slabs], refs[slabs : 2 * slabs], refs[2 * slabs :]
    rows, width = queries[0].shape[1:]
    heads = width // DH
    col = lax.broadcasted_iota(jnp.int32, (1, rows * slabs), 1)
    ones = jnp.ones((rows * slabs, DH), jnp.bfloat16)
    biases = []
    for k in range(NY):
        bias = jnp.full((1, rows * slabs), flags[k * slabs], jnp.float32)
        for j in range(1, slabs):
            bias = jnp.where(col >= j * rows, flags[k * slabs + j], bias)
        biases.append(bias)
    for parity, out in enumerate(outs):
        logs = [[] for _ in range(NY)]
        for h in range(heads):
            lanes = slice(h * DH, (h + 1) * DH)
            q = jnp.concatenate([r[parity, :, lanes] for r in queries], axis=0)
            kk = jnp.concatenate([r[:, lanes] for r in keys], axis=0)
            vv = jnp.concatenate([r[:, lanes] for r in values], axis=0)
            s = lax.dot_general(q, kk, (((1,), (1,)), ((), ())), preferred_element_type=jnp.float32)
            tops, es = [], []
            for k in range(NY):
                part = s[k * rows : (k + 1) * rows] + biases[k]
                top = jnp.max(part, axis=1, keepdims=True)
                es.append(jnp.exp2(part - top).astype(jnp.bfloat16))
                tops.append(top)
            e = jnp.concatenate(es, axis=0)
            o = jnp.dot(e, jnp.concatenate([vv, ones], axis=1), preferred_element_type=jnp.float32)
            for k in range(NY):
                here = slice(k * rows, (k + 1) * rows)
                total = o[here, DH:]
                out[k, 0:rows, lanes] = (o[here, :DH] / total).astype(jnp.bfloat16)
                logs[k].append(tops[k] + jnp.log2(total))
        for k in range(NY):
            out[k, rows : rows + TAIL, 0:rows] = log_rows(logs[k], rows)


def log_rows(columns, rows):
    lane = lax.broadcasted_iota(jnp.int32, (rows, 128), 1)
    tile = jnp.zeros((rows, 128), jnp.float32)
    for j, column in enumerate(columns):
        high = column.astype(jnp.bfloat16).astype(jnp.float32)
        tile = jnp.where(lane == j, high, jnp.where(lane == 8 + j, column - high, tile))
    pick = lax.broadcasted_iota(jnp.int32, (TAIL, 128), 0) == lax.broadcasted_iota(jnp.int32, (TAIL, 128), 1)
    out = lax.dot_general(
        pick.astype(jnp.bfloat16), tile.astype(jnp.bfloat16), (((1,), (1,)), ((), ())), preferred_element_type=jnp.float32
    )
    return out.astype(jnp.bfloat16)


def merge(blocks, rows):
    logs = []
    for block in blocks:
        tail = block[rows : rows + TAIL, 0:rows].astype(jnp.float32)
        logs.append(tail[0:8] + tail[8:16])
    width = blocks[0].shape[1]
    top = functools.reduce(jnp.maximum, logs)
    parts = [jnp.exp2(v - top) for v in logs]
    total = sum(parts)
    inv = 1.0 / total
    row = lax.broadcasted_iota(jnp.int32, (TAIL, width), 0) % 8
    spread = (row == lax.broadcasted_iota(jnp.int32, (TAIL, width), 1) // DH).astype(jnp.bfloat16)
    out = jnp.zeros((rows, width), jnp.float32)
    for part, block in zip(parts, blocks, strict=True):
        weight = part * inv
        high = weight.astype(jnp.bfloat16).astype(jnp.float32)
        both = jnp.concatenate([high, weight - high], axis=0).astype(jnp.bfloat16)
        column = lax.dot_general(both, spread, (((0,), (0,)), ((), ())), preferred_element_type=jnp.float32)
        out = out + column * block[0:rows, :].astype(jnp.float32)
    return out, top + jnp.log2(total)


def pair_kernel(*refs):
    blocks, out = refs[:-1], refs[-1]
    rows = out.shape[1] - TAIL
    for k in range(NY):
        merged, logs = merge([b.at[k] for b in blocks], rows)
        out[k, 0:rows, :] = merged.astype(jnp.bfloat16)
        high = logs.astype(jnp.bfloat16).astype(jnp.float32)
        both = jnp.concatenate([high, logs - high], axis=0)
        out[k, rows : rows + TAIL, 0:rows] = both.astype(jnp.bfloat16)


def out_kernel(x_ref, a, b, c, d, w_ref, *outs):
    rows = a.shape[0] - TAIL
    width = a.shape[1]
    x = x_ref[0]
    merged, _ = merge([a, b, c, d], rows)
    attn = merged.astype(jnp.bfloat16)
    n = len(outs)
    for j in range(n):
        start = pl.multiple_of(lax.rem(x + j, n) * width, 128)
        outs[j][...] = jnp.dot(attn, w_ref[:, pl.ds(start, width)], preferred_element_type=jnp.float32).astype(
            jnp.bfloat16
        )


def shape(dims, dtype):
    return jax.ShapeDtypeStruct(dims, dtype)


def call(kernel, ins, out_shape, flops, moved, exps=0):
    return pl.pallas_call(
        kernel,
        out_shape=out_shape,
        in_specs=ins,
        out_specs=jax.tree.map(lambda _: VMEM, out_shape),
        compiler_params=pltpu.CompilerParams(vmem_limit_bytes=40 * MIB),
        cost_estimate=pl.CostEstimate(flops=flops, bytes_accessed=moved, transcendentals=exps),
    )


def attend(flags, queries, keys, values):
    slots = len(queries)
    rows, width = queries[0].shape[1:]
    slabs = len(keys)
    scores = 2 * slots * rows * rows * slabs * (width // DH)
    return call(
        functools.partial(attend_kernel, slabs),
        [SMEM] + [VMEM] * (slots + 2 * slabs),
        [shape((slots, rows + TAIL, width), jnp.bfloat16)] * 2,
        scores * DH * 14,
        1 << 20,
        scores,
    )(flags, *queries, *keys, *values)


def combine(blocks):
    size = blocks[0].size
    return call(
        pair_kernel, [VMEM] * len(blocks), shape(blocks[0].shape, jnp.bfloat16), size * 2 * len(blocks), size * 2 * len(blocks)
    )(*blocks)


def local(latents, fresh_frame, noise_level, offset, mod_table, w_qkv, w_out, q_gain, k_gain):
    slabs = lax.axis_size("queue")
    frames = slabs // 2
    heads_ax = lax.axis_size("head")
    rows, width = latents.shape
    slab = lax.axis_index("queue")
    x = lax.axis_index("head")
    frame = slab // 2
    z, y = frame // NY, frame % NY
    x_arg = x.astype(jnp.int32).reshape(1)

    def place(f):
        return jnp.mod(f - offset[0], frames)

    chunks = [shift(latents, "head", j) for j in range(1, heads_ax)]
    home_latents = shift(latents, "queue", -2)
    modulation = lax.dynamic_index_in_dim(mod_table, noise_level[place(frame)], 0, keepdims=False)
    home_level = noise_level[place(frame + 1)]
    gate = lax.dynamic_slice(mod_table, (home_level, 2, x * width), (1, 1, width)).reshape(1, width)
    modulation = modulation.reshape(3, heads_ax, 1, width)
    w3 = jnp.transpose(w_qkv, (1, 0, 2))
    w_near = call(early_kernel, [VMEM], shape(w3.shape, jnp.bfloat16), 0, 8 << 20)(w3)
    q, k, v, sums = call(
        project_kernel,
        [SMEM] + [VMEM] * 7,
        [
            shape((rows, width), jnp.float32),
            shape((rows, width), jnp.float32),
            shape((rows, width), jnp.bfloat16),
            shape((8, rows), jnp.float32),
        ],
        2 * rows * D * 3 * width,
        6 << 20,
    )(x_arg, latents, *chunks, modulation[1], modulation[0], w_near)
    all_sums = [sums] + [shift(sums, "head", j) for j in range(1, heads_ax)]
    all_sums, home_latents = lax.optimization_barrier((all_sums, home_latents))
    qn, kn = call(
        norm_kernel,
        [VMEM] * 8,
        [shape((rows, width), jnp.bfloat16)] * 2,
        rows * width * 8,
        2 << 20,
    )(q, k, *all_sums, q_gain.reshape(1, width), k_gain.reshape(1, width))

    def key_route(distance):
        route = []
        for f in range(frames):
            fz, fy = f // NY, f % NY
            source = ((fz - distance) % NZ) * NY + fy
            route += [(2 * source + c, 2 * f + c) for c in range(2)]
        return route

    def y_route(distance):
        route = []
        for f in range(frames):
            fz, fy = f // NY, f % NY
            source = fz * NY + (fy - distance) % NY
            route += [(2 * source + c, 2 * f + c) for c in range(2)]
        return route

    swap = [(i, i ^ 1) for i in range(slabs)]

    def flags_of(distances):
        out = []
        for j in range(NY):
            q_place = place(z * NY + (y + j) % NY + 1)
            for d in distances:
                k_place = place(jnp.mod(z - d, NZ) * NY + y)
                out.append(jnp.where(k_place <= q_place, 0.0, LOW))
        return jnp.stack(out).astype(jnp.float32)

    both = {0: jnp.stack([kn, v])}
    for way in (1, -1):
        both[way] = lax.ppermute(both[0], "queue", key_route(way))
    home_q = [shift(qn, "queue", -2), lax.ppermute(qn, "queue", [((i + 2) % slabs ^ 1, i) for i in range(slabs)])]
    both[1], both[-1], home_q = lax.optimization_barrier((both[1], both[-1], home_q))
    for way in (1, -1):
        both[way * 2] = lax.ppermute(both[way], "queue", key_route(way))
    home_q = jnp.stack(home_q)
    qs = [home_q] + [lax.ppermute(home_q, "queue", y_route(-j)) for j in range(1, NY)]
    for way in (1, -1):
        both[way * 3] = lax.ppermute(both[way * 2], "queue", key_route(way))
    both[3], both[-3], qs = lax.optimization_barrier((both[3], both[-3], qs))
    ks = {d: b[0] for d, b in both.items()}
    vs = {d: b[1] for d, b in both.items()}

    def partial(distances):
        return attend(flags_of(distances), qs, [ks[d] for d in distances], [vs[d] for d in distances])

    ks[4] = lax.ppermute(ks[3], "queue", key_route(1))
    vs[4] = lax.ppermute(vs[-3], "queue", key_route(-1))
    partials = [partial(distances) for distances in GROUPS]
    mine, other = [p[0] for p in partials], [p[1] for p in partials]
    received = lax.ppermute(combine(other), "queue", swap)
    paired = combine(mine + [received])
    parts = [paired[0]] + [lax.ppermute(paired[j], "queue", y_route(j)) for j in range(1, NY)]
    blocks = call(
        out_kernel,
        [SMEM] + [VMEM] * 5,
        [shape((rows, width), jnp.bfloat16)] * heads_ax,
        2 * rows * width * D,
        3 << 20,
    )(x_arg, *parts, w_out)
    proj = blocks[0].astype(jnp.float32)
    for j in range(1, heads_ax):
        proj = proj + shift(blocks[j], "head", j).astype(jnp.float32)
    updated = (home_latents.astype(jnp.float32) + gate * proj).astype(jnp.bfloat16)
    entry_slot = jnp.mod(offset[0] - 1, frames)
    fresh_half = lax.dynamic_slice_in_dim(fresh_frame, slab % 2 * rows, rows, 0)
    return jnp.where(frame == entry_slot, fresh_half, updated)


def solution(mesh):
    return jax.shard_map(
        local,
        mesh=mesh,
        in_specs=(
            P("queue", "head"),
            P(None, "head"),
            P(),
            P(),
            P(),
            P(None, None, "head"),
            P("head", None),
            P("head"),
            P("head"),
        ),
        out_specs=P("queue", "head"),
        check_vma=False,
    )
```
